512 devices in a mesh: grp: 8 (over x, core), ef: 64 (over z, y).
Axes of the slice: x: 4, y: 8, z: 8, core: 2. Of those that a mesh axis runs over, the one named last changes fastest.
Arguments:
- amplitudes: bfloat16 [360000, 512], P('ef', 'grp'), may hold values from -6 to 6
- ladder: bfloat16 [2304, 360000], P('grp', 'ef'), may hold values from -0.01953125 to 0.01953125
- orbital_irrep: int32 [600], replicated, may hold values from 0 to 3
- panel_rows: int32 [2304], P('grp'), may hold values from 0 to 359999
- slot_pair: int32 [64], replicated, may hold values from 0 to 63, each once
Outputs:
- sigma_out: float32 [2304, 512], P('grp', 'ef')
The draws below stay inside these ranges and needn't reach their ends.
Inputs may be any that keep to these rules, and one draw needn't show every extreme that they name: `slot_pair`: each slot holds a different pair.
All inputs are finite; a program needn't handle non-finite values.
Results may differ from the reference program's by a relative error of at most 0.0003.
Values may be sent and summed in bfloat16 or wider, within the bound.
No kernel may reach another device: no remote copies, remote signals or barrier semaphores. Data moves between devices by JAX's collectives and lax.ppermute only.
A program may use at most 64 MiB of HBM per device.

```python
import jax
import jax.numpy as jnp
from jax import lax

V = 600
ROOTS = 8
PAIRS = 64
AB_DEV = 288
AB = 2304
EF = 360000
COLS = 512
N_GRP = 8


def place_ends(result, key, low, high):
    longest = result.shape.index(max(result.shape))
    spots = []
    for shift in (0, 1):
        where = [jax.random.randint(jax.random.fold_in(key, axis), (), 0, length) for axis, length in enumerate(result.shape)]
        where[longest] = (where[longest] + shift) % result.shape[longest]
        spots.append(tuple(where))
    return result.at[spots[0]].set(low).at[spots[1]].set(high)


def block_scale(stream_key, extent, split, low, largest):
    loudness, own = 1.0, jax.random.fold_in(stream_key, 6)
    for position, parts in split:
        draws = jnp.exp(jax.random.uniform(jax.random.fold_in(own, position), (parts,), jnp.float32, low / len(split), largest / len(split)))
        loudness = loudness * jnp.repeat(draws, extent[position] // parts).reshape([-1 if axis == position else 1 for axis in range(len(extent))])
    return loudness


def centred(own_key, shape, scale, bound, split=(), kind=jnp.bfloat16):
    level = block_scale(own_key, shape, split, -0.22, 0.18) if split else 1.0
    entries = jax.random.normal(own_key, shape, jnp.float32) * scale * level
    return jnp.minimum(jnp.maximum(entries, -bound), bound).astype(kind)


def setup_inputs(seed: int = 0) -> dict:
    seeds = jax.random.split(jax.random.key(seed), 6)
    return {
        "amplitudes": centred(seeds[0], (EF, COLS), 1.0, 6.0, ((0, 64), (1, 8))),
        "ladder": centred(seeds[1], (AB, EF), (EF // 4) ** -0.5, 0.01953125, ((0, 8), (1, 64))),
        "orbital_irrep": place_ends(jax.random.randint(seeds[2], (V,), 0, 4), jax.random.fold_in(seeds[2], 1), 0, 3).astype(jnp.int32),
        "panel_rows": place_ends(jax.random.randint(seeds[3], (AB,), 0, V * V), jax.random.fold_in(seeds[3], 1), 0, (V * V) - 1).astype(jnp.int32),
        "slot_pair": jax.random.permutation(seeds[4], PAIRS).astype(jnp.int32),
    }


def reference(amplitudes, ladder, orbital_irrep, panel_rows, slot_pair):
    col_sym = jnp.bitwise_xor(orbital_irrep[:, None], orbital_irrep[None, :]).reshape(V * V)
    row_sym = jnp.bitwise_xor(orbital_irrep[panel_rows // V], orbital_irrep[panel_rows % V])
    blocks = ladder.reshape(N_GRP, AB_DEV, V * V)
    block_sym = row_sym.reshape(N_GRP, AB_DEV)
    zero_val = jnp.zeros((), ladder.dtype)

    def panel_product(items):
        weights, symbols = items
        masked = jnp.where(symbols[:, None] == col_sym[None, :], weights, zero_val)
        return jnp.dot(masked, amplitudes, preferred_element_type=jnp.float32)

    partial_value = lax.map(panel_product, (blocks, block_sym)).reshape(AB, PAIRS, ROOTS)
    sigma_out = jnp.zeros((AB, PAIRS, ROOTS), jnp.float32).at[:, slot_pair, :].set(partial_value)
    return sigma_out.reshape(AB, PAIRS * ROOTS)
```

```python
import jax
import jax.numpy as jnp
from jax import lax
from jax.sharding import PartitionSpec as P

V = 600
ROOTS = 8
N_X = 4


def lookup(indices, orbital_irrep):
    orbitals = jnp.arange(orbital_irrep.shape[0], dtype=jnp.int32)
    return jnp.max(
        jnp.where(indices[:, None] == orbitals[None, :], orbital_irrep[None, :], 0), axis=1
    )


def column_symmetry(orbital_irrep, width):
    offset = lax.axis_index("ef") * width
    count = (V - 1 + width) // V + 1
    first = offset // V
    padded = jnp.concatenate([orbital_irrep, jnp.zeros((count,), jnp.int32)])
    outer = lax.dynamic_slice(padded, (first,), (count,))
    table = jnp.bitwise_xor(outer[:, None], orbital_irrep[None, :]).reshape(count * V)
    return lax.dynamic_slice(table, (offset - first * V,), (width,))


def along_x(value, step):
    pairs = [
        (x * 2 + c, (x + step) % N_X * 2 + c) for x in range(N_X) for c in range(2)
    ]
    return lax.ppermute(value, "grp", pairs)


def other_core(value):
    return lax.ppermute(value, "grp", [(g, g ^ 1) for g in range(2 * N_X)])


def product(columns, rows):
    return lax.dot_general(
        columns, rows, (((1,), (1,)), ((), ())), preferred_element_type=jnp.float32
    )


def on_device(amplitudes, ladder, orbital_irrep, panel_rows, slot_pair):
    width = ladder.shape[1]
    rows = ladder.shape[0]
    pairs = slot_pair.shape[0]
    own = amplitudes.T
    half = own.shape[0] // 2
    low, high = own[:half], own[half:]
    left_low = along_x(low, 1)
    right_high = along_x(high, -1)
    left_high = along_x(high, 1)
    right_low = along_x(low, -1)
    far_low = along_x(left_low, 1)
    far_high = along_x(right_high, -1)

    col_sym = column_symmetry(orbital_irrep, width)
    row_sym = jnp.bitwise_xor(
        lookup(panel_rows // V, orbital_irrep), lookup(panel_rows % V, orbital_irrep)
    )
    masked = jnp.where(row_sym[:, None] == col_sym[None, :], ladder, jnp.zeros((), ladder.dtype))
    masked_other = other_core(masked)

    near = [own, left_low, left_high, right_low, right_high]
    far = [far_low, far_high]
    near_other = other_core(jnp.concatenate([product(c, masked_other) for c in near]))
    near_own = [product(c, masked) for c in near]
    far_other = other_core(jnp.concatenate([product(c, masked_other) for c in far]))
    far_own = [product(c, masked) for c in far]
    blocks = jnp.concatenate(near_own + far_own + [near_other, far_other])
    blocks = blocks.reshape(pairs, ROOTS, rows)

    grp = lax.axis_index("grp")
    x, c = grp // 2, grp % 2
    chips = jnp.stack([x, (x + N_X - 1) % N_X, (x + 1) % N_X, (x + 2) % N_X])
    cores = jnp.stack([c, 1 - c])
    groups = (chips[None, :] * 2 + cores[:, None]).reshape(-1)
    held = slot_pair.reshape(2 * N_X, -1)[groups].reshape(-1)
    order = jnp.argmax(held[None, :] == jnp.arange(pairs, dtype=jnp.int32)[:, None], axis=1)
    ordered = jnp.take(blocks, order, axis=0)
    received = lax.all_to_all(ordered, "ef", 0, 0, tiled=True)
    return jnp.sum(received, axis=0).T


def solution(mesh):
    in_specs = (P("ef", "grp"), P("grp", "ef"), P(), P("grp"), P())
    out_specs = P("grp", "ef")
    return jax.shard_map(
        on_device, mesh=mesh, in_specs=in_specs, out_specs=out_specs, check_vma=False
    )
```

```python
import functools

import jax
import jax.numpy as jnp
from jax import lax
from jax.experimental import pallas as pl
from jax.experimental.pallas import tpu as pltpu
from jax.sharding import PartitionSpec as P

V = 600
ROOTS = 8
N_X = 4
GROUP_SLOTS = 8
CHUNK = 1024
LANES = 128
TAIL = 32
VMEM_LIMIT = 10 << 20

VMEM = pl.BlockSpec(memory_space=pltpu.VMEM)
HBM = pl.BlockSpec(memory_space=pltpu.HBM)
SMEM = pl.BlockSpec(memory_space=pltpu.SMEM)


def lookup(indices, orbital_irrep):
    orbitals = jnp.arange(orbital_irrep.shape[0], dtype=jnp.int32)
    return jnp.max(
        jnp.where(indices[:, None] == orbitals[None, :], orbital_irrep[None, :], 0), axis=1
    )


def column_symmetry(orbital_irrep, width):
    offset = lax.axis_index("ef") * width
    count = (V - 1 + width) // V + 1
    first = offset // V
    padded = jnp.concatenate([orbital_irrep, jnp.zeros((count,), jnp.int32)])
    outer = lax.dynamic_slice(padded, (first,), (count,))
    table = jnp.bitwise_xor(outer[:, None], orbital_irrep[None, :]).reshape(count * V)
    return lax.dynamic_slice(table, (offset - first * V,), (width,))


def neighbour(x, c):
    return (N_X - 1 - x) * c + (x + 1 - 2 * (x % 2)) * (1 - c)


def other_chip(value, link):
    pairs = [(x * 2 + c, neighbour(x, c ^ link) * 2 + c) for x in range(N_X) for c in range(2)]
    return lax.ppermute(value, "grp", pairs)


def other_core(value):
    return lax.ppermute(value, "grp", [(g, g ^ 1) for g in range(2 * N_X)])


def product(columns, rows):
    width = rows.shape[1]
    total = None
    for low in range(0, width, CHUNK):
        span = slice(low, min(low + CHUNK, width))
        left = jnp.concatenate([c[:, span] for c in columns], axis=0)
        part = lax.dot_general(
            left, rows[:, span], (((1,), (1,)), ((), ())), preferred_element_type=jnp.float32
        )
        total = part if total is None else total + part
    return total


def pack(out, pair, source, base):
    block = source[pl.ds(base, ROOTS), :]
    for j in range(ROOTS // 2):
        two = slice(2 * j, 2 * j + 2)
        out[pair, :, j * LANES : (j + 1) * LANES] = block[two, :LANES]
        out[pair, :, (4 + j) * LANES : (5 + j) * LANES] = block[two, LANES : 2 * LANES]
    lane = lax.broadcasted_iota(jnp.int32, (2, LANES), 1)
    tail = block[:2, 2 * LANES :]
    for j in range(1, ROOTS // 2):
        piece = pltpu.roll(block[2 * j : 2 * j + 2, 2 * LANES :], j * TAIL, 1)
        tail = jnp.where(lane >= j * TAIL, piece, tail)
    out[pair, :, 8 * LANES :] = tail


def store_slots(grp, slot_pair, owners, held, out):
    for block, (chip, core) in enumerate(owners):
        group = lax.rem(chip, N_X) * 2 + core
        for slot in range(GROUP_SLOTS):
            pair = slot_pair[group * GROUP_SLOTS + slot]
            pack(out, pair, held, (block * GROUP_SLOTS + slot) * ROOTS)


def owners_of(grp, part):
    x, c = grp[0] // 2, grp[0] % 2
    if part == "chip":
        return (x, c), (x, 1 - c)
    if part == "near":
        a, b = neighbour(x, c), neighbour(x, 1 - c)
        return (a, c), (b, 1 - c), (b, c), (a, 1 - c)
    return (x + 2, c), (x + 2, 1 - c)


def fetching_kernel(part, grp, slot_pair, rows, *refs):
    owners = owners_of(grp, part)
    count = len(owners)
    sources, out = refs[:count], refs[-count - 3]
    *fetched, held, sems = refs[-count - 2 :]
    copies = [
        pltpu.make_async_copy(source, target, sems.at[i])
        for i, (source, target) in enumerate(zip(sources, fetched, strict=True))
    ]
    for copy in copies:
        copy.start()
    for copy in copies:
        copy.wait()
    held[:, : rows.shape[0]] = product(fetched, rows)
    store_slots(grp, slot_pair, owners, held, out)


def far_kernel(grp, slot_pair, rows, far, far_other, near, out, held):
    held[:, : rows.shape[0]] = product((far, far_other), rows)
    store_slots(grp, slot_pair, owners_of(grp, "far"), held, out)


def estimate(columns, rows):
    count = sum(c.shape[0] for c in columns)
    return pl.CostEstimate(
        flops=8 * count * rows.shape[0] * rows.shape[1],
        bytes_accessed=2 * rows.shape[1] * (count + rows.shape[0]),
        transcendentals=0,
    )


def slot_products(part, grp, slot_pair, rows, columns, ordered=None):
    count = sum(c.shape[0] for c in columns)
    held = [pltpu.VMEM((count, 3 * LANES), jnp.float32)]
    if part == "far":
        kernel, place, scratch = far_kernel, VMEM, held
    else:
        kernel, place = functools.partial(fetching_kernel, part), HBM
        scratch = [pltpu.VMEM(c.shape, c.dtype) for c in columns] + held
        scratch.append(pltpu.SemaphoreType.DMA((len(columns),)))
    before = [] if ordered is None else [ordered]
    return pl.pallas_call(
        kernel,
        out_shape=jax.ShapeDtypeStruct((slot_pair.shape[0], 2, 9 * LANES), jnp.float32),
        in_specs=[SMEM, SMEM, VMEM] + [place] * len(columns) + [VMEM] * len(before),
        out_specs=VMEM,
        scratch_shapes=scratch,
        input_output_aliases={3 + len(columns): 0} if before else {},
        compiler_params=pltpu.CompilerParams(vmem_limit_bytes=VMEM_LIMIT),
        cost_estimate=estimate(columns, rows),
    )(grp, slot_pair, rows, *columns, *before)


def total_kernel(received, out):
    total = jnp.sum(received[...], axis=0)
    for j in range(ROOTS // 2):
        two = slice(2 * j, 2 * j + 2)
        out[two, :LANES] = total[:, j * LANES : (j + 1) * LANES]
        out[two, LANES : 2 * LANES] = total[:, (4 + j) * LANES : (5 + j) * LANES]
        tail = total[:, 8 * LANES :]
        tail = tail if j == 0 else pltpu.roll(tail, LANES - j * TAIL, 1)
        out[two, 2 * LANES :] = tail[:, :TAIL]


def add_received(received, rows):
    return pl.pallas_call(
        total_kernel,
        out_shape=jax.ShapeDtypeStruct((ROOTS, rows), jnp.float32),
        in_specs=[VMEM],
        out_specs=VMEM,
        compiler_params=pltpu.CompilerParams(vmem_limit_bytes=VMEM_LIMIT),
    )(received)


def on_device(amplitudes, ladder, orbital_irrep, panel_rows, slot_pair):
    grp = lax.axis_index("grp").astype(jnp.int32).reshape(1)
    own = amplitudes.T
    mine = other_chip(own, 0)

    col_sym = column_symmetry(orbital_irrep, ladder.shape[1])
    row_sym = jnp.bitwise_xor(
        lookup(panel_rows // V, orbital_irrep), lookup(panel_rows % V, orbital_irrep)
    )
    masked = jnp.where(row_sym[:, None] == col_sym[None, :], ladder, jnp.zeros((), ladder.dtype))
    later, masked = lax.optimization_barrier((own, masked))
    theirs = other_chip(later, 1)

    own_other = other_core(own)
    ordered = slot_products("chip", grp, slot_pair, masked, (own, own_other))
    mine, ordered = lax.optimization_barrier((mine, ordered))
    far = other_chip(mine, 1)
    mine_late, theirs = lax.optimization_barrier((mine, theirs))
    mine_other, theirs_other = other_core(mine_late), other_core(theirs)
    near = (mine, mine_other, theirs, theirs_other)
    ordered = slot_products("near", grp, slot_pair, masked, near, ordered)
    far_other = other_core(far)
    ordered = slot_products("far", grp, slot_pair, masked, (far, far_other), ordered)
    received = lax.all_to_all(ordered, "ef", 0, 0, tiled=True)
    return add_received(received, ladder.shape[0]).T


def solution(mesh):
    in_specs = (P("ef", "grp"), P("grp", "ef"), P(), P("grp"), P())
    out_specs = P("grp", "ef")
    return jax.shard_map(
        on_device, mesh=mesh, in_specs=in_specs, out_specs=out_specs, check_vma=False
    )
```

```python
import functools

import jax
import jax.numpy as jnp
from jax import lax
from jax.experimental import pallas as pl
from jax.experimental.pallas import tpu as pltpu
from jax.sharding import PartitionSpec as P

V = 600
ROOTS = 8
N_X = 4
GROUP_SLOTS = 8
CHUNK = 1024
LANES = 128
TAIL = 32
STEPS = 32000.0
SMALLEST = 1e-30
VMEM_LIMIT = 10 << 20

VMEM = pl.BlockSpec(memory_space=pltpu.VMEM)
SMEM = pl.BlockSpec(memory_space=pltpu.SMEM)


def lookup(indices, orbital_irrep):
    orbitals = jnp.arange(orbital_irrep.shape[0], dtype=jnp.int32)
    return jnp.max(
        jnp.where(indices[:, None] == orbitals[None, :], orbital_irrep[None, :], 0), axis=1
    )


def column_symmetry(orbital_irrep, width):
    offset = lax.axis_index("ef") * width
    count = (V - 1 + width) // V + 1
    first = offset // V
    padded = jnp.concatenate([orbital_irrep, jnp.zeros((count,), jnp.int32)])
    outer = lax.dynamic_slice(padded, (first,), (count,))
    table = jnp.bitwise_xor(outer[:, None], orbital_irrep[None, :]).reshape(count * V)
    return lax.dynamic_slice(table, (offset - first * V,), (width,))


def neighbour(x, c):
    return (N_X - 1 - x) * c + (x + 1 - 2 * (x % 2)) * (1 - c)


def other_chip(value, link):
    pairs = [(x * 2 + c, neighbour(x, c ^ link) * 2 + c) for x in range(N_X) for c in range(2)]
    return lax.ppermute(value, "grp", pairs)


def other_core(value):
    return lax.ppermute(value, "grp", [(g, g ^ 1) for g in range(2 * N_X)])


def product(columns, rows):
    width = rows.shape[1]
    total = None
    for low in range(0, width, CHUNK):
        span = slice(low, min(low + CHUNK, width))
        left = jnp.concatenate([c[:, span] for c in columns], axis=0)
        part = lax.dot_general(
            left, rows[:, span], (((1,), (1,)), ((), ())), preferred_element_type=jnp.float32
        )
        total = part if total is None else total + part
    return total


def pack(out, pair, block, exponent):
    for j in range(ROOTS // 2):
        two = slice(2 * j, 2 * j + 2)
        out[pair, :, j * LANES : (j + 1) * LANES] = block[two, :LANES]
        out[pair, :, (4 + j) * LANES : (5 + j) * LANES] = block[two, LANES : 2 * LANES]
    lane = lax.broadcasted_iota(jnp.int32, (2, LANES), 1)
    tail = block[:2, 2 * LANES :]
    for j in range(1, ROOTS // 2):
        piece = pltpu.roll(block[2 * j : 2 * j + 2, 2 * LANES :], j * TAIL, 1)
        tail = jnp.where(lane >= j * TAIL, piece, tail)
    out[pair, :, 8 * LANES : 9 * LANES] = tail
    out[pair, :, 9 * LANES :] = exponent


def store_slots(grp, slot_pair, owners, held, steps, exponents, out):
    count = held.shape[0] // ROOTS
    values = held[...].reshape(count, ROOTS, held.shape[1])
    largest = jnp.max(jnp.max(jnp.abs(values), axis=1, keepdims=True), axis=2, keepdims=True)
    exponent = jnp.floor(jnp.log2(jnp.maximum(largest, SMALLEST))) + 1.0
    scale = jnp.exp2(-exponent) * STEPS
    steps[...] = jnp.round(values * scale).astype(jnp.int32)
    exponents[...] = jnp.broadcast_to(exponent, exponents.shape).astype(jnp.int32)
    for block, (chip, core) in enumerate(owners):
        group = lax.rem(chip, N_X) * 2 + core
        for slot in range(GROUP_SLOTS):
            pair = slot_pair[group * GROUP_SLOTS + slot]
            index = block * GROUP_SLOTS + slot
            pack(out, pair, steps[index], exponents[index])


def owners_of(grp, part):
    x, c = grp[0] // 2, grp[0] % 2
    a, b = neighbour(x, c), neighbour(x, 1 - c)
    if part == "first":
        return (x, c), (x, 1 - c), (a, c)
    if part == "second":
        return (b, c), (b, 1 - c), (a, 1 - c)
    return (x + 2, c), (x + 2, 1 - c)


def product_kernel(part, grp, slot_pair, rows, *refs):
    owners = owners_of(grp, part)
    out, held, steps, exponents = refs[-4:]
    count = rows.shape[0]
    held[:, 2 * LANES :] = jnp.zeros((held.shape[0], LANES), held.dtype)
    held[:, :count] = product(refs[: len(owners)], rows)
    store_slots(grp, slot_pair, owners, held, steps, exponents, out)


def estimate(columns, rows):
    count = sum(c.shape[0] for c in columns)
    return pl.CostEstimate(
        flops=8 * count * rows.shape[0] * rows.shape[1],
        bytes_accessed=2 * rows.shape[1] * (count + rows.shape[0]),
        transcendentals=0,
    )


def slot_products(part, grp, slot_pair, rows, columns, ordered=None):
    count = sum(c.shape[0] for c in columns)
    before = [] if ordered is None else [ordered]
    return pl.pallas_call(
        functools.partial(product_kernel, part),
        out_shape=jax.ShapeDtypeStruct((slot_pair.shape[0], 2, 10 * LANES), jnp.int32),
        in_specs=[SMEM, SMEM, VMEM] + [VMEM] * len(columns) + [VMEM] * len(before),
        out_specs=VMEM,
        scratch_shapes=[
            pltpu.VMEM((count, 3 * LANES), jnp.float32),
            pltpu.VMEM((count // ROOTS, ROOTS, 3 * LANES), jnp.int32),
            pltpu.VMEM((count // ROOTS, 2, LANES), jnp.int32),
        ],
        input_output_aliases={3 + len(columns): 0} if before else {},
        compiler_params=pltpu.CompilerParams(vmem_limit_bytes=VMEM_LIMIT),
        cost_estimate=estimate(columns, rows),
    )(grp, slot_pair, rows, *columns, *before)


def total_kernel(received, out):
    width = 9 * LANES
    unit = jnp.exp2(received[:, :, width:].astype(jnp.float32)) * (1.0 / STEPS)
    for j in range(9):
        steps = received[:, :, j * LANES : (j + 1) * LANES].astype(jnp.float32)
        total = jnp.sum(steps * unit, axis=0)
        if j < 8:
            row = 2 * (j % 4)
            out[row : row + 2, j // 4 * LANES : (j // 4 + 1) * LANES] = total
        else:
            for i in range(ROOTS // 2):
                tail = total if i == 0 else pltpu.roll(total, LANES - i * TAIL, 1)
                out[2 * i : 2 * i + 2, 2 * LANES :] = tail[:, :TAIL]


def add_received(received, rows):
    return pl.pallas_call(
        total_kernel,
        out_shape=jax.ShapeDtypeStruct((ROOTS, rows), jnp.float32),
        in_specs=[VMEM],
        out_specs=VMEM,
        compiler_params=pltpu.CompilerParams(vmem_limit_bytes=VMEM_LIMIT),
    )(received)


def on_device(amplitudes, ladder, orbital_irrep, panel_rows, slot_pair):
    grp = lax.axis_index("grp").astype(jnp.int32).reshape(1)
    own = amplitudes.T
    mine = other_chip(own, 0)

    col_sym = column_symmetry(orbital_irrep, ladder.shape[1])
    row_sym = jnp.bitwise_xor(
        lookup(panel_rows // V, orbital_irrep), lookup(panel_rows % V, orbital_irrep)
    )
    first, row_sym, col_sym = lax.optimization_barrier((own, row_sym, col_sym))
    theirs, own_other = other_chip(first, 1), other_core(first)
    mine, row_sym, col_sym = lax.optimization_barrier((mine, row_sym, col_sym))
    far = other_chip(mine, 1)
    masked = jnp.where(row_sym[:, None] == col_sym[None, :], ladder, jnp.zeros((), ladder.dtype))
    ordered = slot_products("first", grp, slot_pair, masked, (own, own_other, mine))
    mine, theirs, ordered = lax.optimization_barrier((mine, theirs, ordered))
    mine_other, theirs_other = other_core(mine), other_core(theirs)
    near = (theirs, mine_other, theirs_other)
    ordered = slot_products("second", grp, slot_pair, masked, near, ordered)
    far_other = other_core(far)
    ordered = slot_products("far", grp, slot_pair, masked, (far, far_other), ordered)
    received = lax.all_to_all(ordered.astype(jnp.int16), "ef", 0, 0, tiled=True)
    return add_received(received.astype(jnp.int32), ladder.shape[0]).T


def solution(mesh):
    in_specs = (P("ef", "grp"), P("grp", "ef"), P(), P("grp"), P())
    out_specs = P("grp", "ef")
    return jax.shard_map(
        on_device, mesh=mesh, in_specs=in_specs, out_specs=out_specs, check_vma=False
    )
```

```python
import functools

import jax
import jax.numpy as jnp
from jax import lax
from jax.experimental import pallas as pl
from jax.experimental.pallas import tpu as pltpu
from jax.sharding import PartitionSpec as P

V = 600
ROOTS = 8
N_X = 4
GROUP_SLOTS = 8
CHUNK = 1024
LANES = 128
TAIL = 32
STEPS = 32000.0
SMALLEST = 1e-30
VMEM_LIMIT = 10 << 20

VMEM = pl.BlockSpec(memory_space=pltpu.VMEM)
SMEM = pl.BlockSpec(memory_space=pltpu.SMEM)


def lookup(indices, orbital_irrep):
    orbitals = jnp.arange(orbital_irrep.shape[0], dtype=jnp.int32)
    return jnp.max(
        jnp.where(indices[:, None] == orbitals[None, :], orbital_irrep[None, :], 0), axis=1
    )


def copy_kernel(*refs):
    for source, out in zip(refs[: len(refs) // 2], refs[len(refs) // 2 :], strict=True):
        out[...] = source[...]


def near_copies(*tables):
    return pl.pallas_call(
        copy_kernel,
        out_shape=[jax.ShapeDtypeStruct(t.shape, t.dtype) for t in tables],
        in_specs=[VMEM] * len(tables),
        out_specs=[VMEM] * len(tables),
        compiler_params=pltpu.CompilerParams(vmem_limit_bytes=VMEM_LIMIT),
        cost_estimate=pl.CostEstimate(flops=0, bytes_accessed=4096, transcendentals=0),
    )(*tables)


def column_symmetry(orbital_irrep, width):
    offset = lax.axis_index("ef") * width
    count = (V - 1 + width) // V + 1
    first = offset // V
    padded = jnp.concatenate([orbital_irrep, jnp.zeros((count,), jnp.int32)])
    outer = lax.dynamic_slice(padded, (first,), (count,))
    table = jnp.bitwise_xor(outer[:, None], orbital_irrep[None, :]).reshape(count * V)
    return lax.dynamic_slice(table, (offset - first * V,), (width,))


def neighbour(x, c):
    return (N_X - 1 - x) * c + (x + 1 - 2 * (x % 2)) * (1 - c)


def other_chip(value, link):
    pairs = [(x * 2 + c, neighbour(x, c ^ link) * 2 + c) for x in range(N_X) for c in range(2)]
    return lax.ppermute(value, "grp", pairs)


def other_core(value):
    return lax.ppermute(value, "grp", [(g, g ^ 1) for g in range(2 * N_X)])


def product(columns, rows):
    width = rows.shape[1]
    total = None
    for low in range(0, width, CHUNK):
        span = slice(low, min(low + CHUNK, width))
        left = jnp.concatenate([c[:, span] for c in columns], axis=0)
        part = lax.dot_general(
            rows[:, span], left, (((1,), (1,)), ((), ())), preferred_element_type=jnp.float32
        )
        total = part if total is None else total + part
    return total.T


def pack(out, pair, block, exponent):
    lane = lax.broadcasted_iota(jnp.int32, (2, LANES), 1)
    tail = block[:2, 2 * LANES :]
    for j in range(1, ROOTS // 2):
        piece = pltpu.roll(block[2 * j : 2 * j + 2, 2 * LANES :], j * TAIL, 1)
        tail = jnp.where(lane >= j * TAIL, piece, tail)
    pieces = [block[2 * j : 2 * j + 2, :LANES] for j in range(ROOTS // 2)]
    pieces += [block[2 * j : 2 * j + 2, LANES : 2 * LANES] for j in range(ROOTS // 2)]
    out[pair] = jnp.concatenate(pieces + [tail, exponent], axis=1).astype(out.dtype)


def store_slots(grp, slot_pair, owners, held, steps, exponents, out):
    count = held.shape[0] // ROOTS
    values = held[...].reshape(count, ROOTS, held.shape[1])
    largest = jnp.max(jnp.max(jnp.abs(values), axis=1, keepdims=True), axis=2, keepdims=True)
    exponent = jnp.floor(jnp.log2(jnp.maximum(largest, SMALLEST))) + 1.0
    scale = jnp.exp2(-exponent) * STEPS
    steps[...] = jnp.round(values * scale).astype(jnp.int32)
    exponents[...] = jnp.broadcast_to(exponent, exponents.shape).astype(jnp.int32)
    for block, (chip, core) in enumerate(owners):
        group = lax.rem(chip, N_X) * 2 + core
        for slot in range(GROUP_SLOTS):
            pair = slot_pair[group * GROUP_SLOTS + slot]
            index = block * GROUP_SLOTS + slot
            pack(out, pair, steps[index], exponents[index])


def owners_of(grp, part):
    x, c = grp[0] // 2, grp[0] % 2
    a, b = neighbour(x, c), neighbour(x, 1 - c)
    if part == "first":
        return (x, c), (x, 1 - c), (a, c)
    if part == "second":
        return (b, c), (b, 1 - c), (a, 1 - c)
    return (x + 2, c), (x + 2, 1 - c)


def product_kernel(part, grp, slot_pair, rows, *refs):
    owners = owners_of(grp, part)
    out, held, steps, exponents = refs[-4:]
    count = rows.shape[0]
    held[:, 2 * LANES :] = jnp.zeros((held.shape[0], LANES), held.dtype)
    held[:, :count] = product(refs[: len(owners)], rows)
    store_slots(grp, slot_pair, owners, held, steps, exponents, out)


def estimate(columns, rows):
    count = sum(c.shape[0] for c in columns)
    return pl.CostEstimate(
        flops=8 * count * rows.shape[0] * rows.shape[1],
        bytes_accessed=2 * rows.shape[1] * (count + rows.shape[0]),
        transcendentals=0,
    )


def slot_products(part, grp, slot_pair, rows, columns, ordered=None):
    count = sum(c.shape[0] for c in columns)
    before = [] if ordered is None else [ordered]
    return pl.pallas_call(
        functools.partial(product_kernel, part),
        out_shape=jax.ShapeDtypeStruct((slot_pair.shape[0], 2, 10 * LANES), jnp.int16),
        in_specs=[SMEM, SMEM, VMEM] + [VMEM] * len(columns) + [VMEM] * len(before),
        out_specs=VMEM,
        scratch_shapes=[
            pltpu.VMEM((count, 3 * LANES), jnp.float32),
            pltpu.VMEM((count // ROOTS, ROOTS, 3 * LANES), jnp.int32),
            pltpu.VMEM((count // ROOTS, 2, LANES), jnp.int32),
        ],
        input_output_aliases={3 + len(columns): 0} if before else {},
        compiler_params=pltpu.CompilerParams(vmem_limit_bytes=VMEM_LIMIT),
        cost_estimate=estimate(columns, rows),
    )(grp, slot_pair, rows, *columns, *before)


def total_kernel(received, out):
    width = 9 * LANES
    unit = jnp.exp2(received[:, :, width:].astype(jnp.int32).astype(jnp.float32)) * (1.0 / STEPS)
    for j in range(9):
        steps = received[:, :, j * LANES : (j + 1) * LANES].astype(jnp.int32).astype(jnp.float32)
        total = jnp.sum(steps * unit, axis=0)
        if j < 8:
            row = 2 * (j % 4)
            out[row : row + 2, j // 4 * LANES : (j // 4 + 1) * LANES] = total
        else:
            for i in range(ROOTS // 2):
                tail = total if i == 0 else pltpu.roll(total, LANES - i * TAIL, 1)
                out[2 * i : 2 * i + 2, 2 * LANES :] = tail[:, :TAIL]


def add_received(received, rows):
    return pl.pallas_call(
        total_kernel,
        out_shape=jax.ShapeDtypeStruct((ROOTS, rows), jnp.float32),
        in_specs=[VMEM],
        out_specs=VMEM,
        compiler_params=pltpu.CompilerParams(vmem_limit_bytes=VMEM_LIMIT),
    )(received)


def on_device(amplitudes, ladder, orbital_irrep, panel_rows, slot_pair):
    grp = lax.axis_index("grp").astype(jnp.int32).reshape(1)
    own = amplitudes.T
    mine = other_chip(own, 0)

    orbital_irrep, panel_rows = near_copies(orbital_irrep, panel_rows)
    col_sym = column_symmetry(orbital_irrep, ladder.shape[1])
    row_sym = jnp.bitwise_xor(
        lookup(panel_rows // V, orbital_irrep), lookup(panel_rows % V, orbital_irrep)
    )
    first, row_sym, col_sym = lax.optimization_barrier((own, row_sym, col_sym))
    theirs, own_other = other_chip(first, 1), other_core(first)
    mine, row_sym, col_sym = lax.optimization_barrier((mine, row_sym, col_sym))
    far = other_chip(mine, 1)
    masked = jnp.where(row_sym[:, None] == col_sym[None, :], ladder, jnp.zeros((), ladder.dtype))
    ordered = slot_products("first", grp, slot_pair, masked, (own, own_other, mine))
    mine, theirs, ordered = lax.optimization_barrier((mine, theirs, ordered))
    mine_other, theirs_other = other_core(mine), other_core(theirs)
    near = (theirs, mine_other, theirs_other)
    ordered = slot_products("second", grp, slot_pair, masked, near, ordered)
    far_other = other_core(far)
    ordered = slot_products("far", grp, slot_pair, masked, (far, far_other), ordered)
    received = lax.all_to_all(ordered, "ef", 0, 0, tiled=True)
    return add_received(received, ladder.shape[0]).T


def solution(mesh):
    in_specs = (P("ef", "grp"), P("grp", "ef"), P(), P("grp"), P())
    out_specs = P("grp", "ef")
    return jax.shard_map(
        on_device, mesh=mesh, in_specs=in_specs, out_specs=out_specs, check_vma=False
    )
```

```python
import functools

import jax
import jax.numpy as jnp
from jax import lax
from jax.experimental import pallas as pl
from jax.experimental.pallas import tpu as pltpu
from jax.sharding import PartitionSpec as P

V = 600
ROOTS = 8
N_X = 4
GROUP_SLOTS = 8
CHUNK = 1024
LANES = 128
TAIL = 32
STEPS = 32000.0
SMALLEST = 1e-30
VMEM_LIMIT = 10 << 20

VMEM = pl.BlockSpec(memory_space=pltpu.VMEM)
SMEM = pl.BlockSpec(memory_space=pltpu.SMEM)


def lookup(indices, orbital_irrep):
    orbitals = jnp.arange(orbital_irrep.shape[0], dtype=jnp.int32)
    return jnp.max(
        jnp.where(indices[:, None] == orbitals[None, :], orbital_irrep[None, :], 0), axis=1
    )


def copy_kernel(*refs):
    for source, out in zip(refs[: len(refs) // 2], refs[len(refs) // 2 :], strict=True):
        out[...] = source[...]


def near_copies(*tables):
    return pl.pallas_call(
        copy_kernel,
        out_shape=[jax.ShapeDtypeStruct(t.shape, t.dtype) for t in tables],
        in_specs=[VMEM] * len(tables),
        out_specs=[VMEM] * len(tables),
        compiler_params=pltpu.CompilerParams(vmem_limit_bytes=VMEM_LIMIT),
        cost_estimate=pl.CostEstimate(flops=0, bytes_accessed=4096, transcendentals=0),
    )(*tables)


def column_symmetry(orbital_irrep, width):
    offset = lax.axis_index("ef") * width
    count = (V - 1 + width) // V + 1
    first = offset // V
    padded = jnp.concatenate([orbital_irrep, jnp.zeros((count,), jnp.int32)])
    outer = lax.dynamic_slice(padded, (first,), (count,))
    table = jnp.bitwise_xor(outer[:, None], orbital_irrep[None, :]).reshape(count * V)
    return lax.dynamic_slice(table, (offset - first * V,), (width,))


def neighbour(x, c):
    return (N_X - 1 - x) * c + (x + 1 - 2 * (x % 2)) * (1 - c)


def other_chip(value, link):
    pairs = [(x * 2 + c, neighbour(x, c ^ link) * 2 + c) for x in range(N_X) for c in range(2)]
    return lax.ppermute(value, "grp", pairs)


def other_core(value):
    return lax.ppermute(value, "grp", [(g, g ^ 1) for g in range(2 * N_X)])


def product(columns, rows):
    width = rows.shape[1]
    total = None
    for low in range(0, width, CHUNK):
        span = slice(low, min(low + CHUNK, width))
        left = jnp.concatenate([c[:, span] for c in columns], axis=0)
        part = lax.dot_general(
            rows[:, span], left, (((1,), (1,)), ((), ())), preferred_element_type=jnp.float32
        )
        total = part if total is None else total + part
    return total.T


def pack(out, pair, block, exponent):
    lane = lax.broadcasted_iota(jnp.int32, (2, LANES), 1)
    tail = block[:2, 2 * LANES :]
    for j in range(1, ROOTS // 2):
        piece = pltpu.roll(block[2 * j : 2 * j + 2, 2 * LANES :], j * TAIL, 1)
        tail = jnp.where(lane >= j * TAIL, piece, tail)
    pieces = [block[2 * j : 2 * j + 2, :LANES] for j in range(ROOTS // 2)]
    pieces += [block[2 * j : 2 * j + 2, LANES : 2 * LANES] for j in range(ROOTS // 2)]
    out[pair] = jnp.concatenate(pieces + [tail, exponent], axis=1).astype(out.dtype)


def store_slots(grp, slot_pair, owners, held, steps, exponents, out):
    count = held.shape[0] // ROOTS
    values = held[...].reshape(count, ROOTS, held.shape[1])
    largest = jnp.max(jnp.max(jnp.abs(values), axis=1, keepdims=True), axis=2, keepdims=True)
    exponent = jnp.floor(jnp.log2(jnp.maximum(largest, SMALLEST))) + 1.0
    scale = jnp.exp2(-exponent) * STEPS
    steps[...] = jnp.round(values * scale).astype(jnp.int32)
    exponents[...] = jnp.broadcast_to(exponent, exponents.shape).astype(jnp.int32)
    for block, (chip, core) in enumerate(owners):
        group = lax.rem(chip, N_X) * 2 + core
        for slot in range(GROUP_SLOTS):
            pair = slot_pair[group * GROUP_SLOTS + slot]
            index = block * GROUP_SLOTS + slot
            pack(out, pair, steps[index], exponents[index])


def owners_of(grp, part):
    x, c = grp[0] // 2, grp[0] % 2
    a, b = neighbour(x, c), neighbour(x, 1 - c)
    if part == "first":
        return (x, c), (x, 1 - c), (a, c)
    if part == "second":
        return (b, c), (b, 1 - c), (a, 1 - c)
    return (x + 2, c), (x + 2, 1 - c)


def product_kernel(part, grp, slot_pair, rows, *refs):
    owners = owners_of(grp, part)
    out, held, steps, exponents = refs[-4:]
    count = rows.shape[0]
    held[:, 2 * LANES :] = jnp.zeros((held.shape[0], LANES), held.dtype)
    held[:, :count] = product(refs[: len(owners)], rows)
    store_slots(grp, slot_pair, owners, held, steps, exponents, out)


def estimate(columns, rows):
    count = sum(c.shape[0] for c in columns)
    return pl.CostEstimate(
        flops=8 * count * rows.shape[0] * rows.shape[1],
        bytes_accessed=2 * rows.shape[1] * (count + rows.shape[0]),
        transcendentals=0,
    )


def slot_products(part, grp, slot_pair, rows, columns, ordered=None):
    count = sum(c.shape[0] for c in columns)
    before = [] if ordered is None else [ordered]
    return pl.pallas_call(
        functools.partial(product_kernel, part),
        out_shape=jax.ShapeDtypeStruct((slot_pair.shape[0], 2, 10 * LANES), jnp.int16),
        in_specs=[SMEM, SMEM, VMEM] + [VMEM] * len(columns) + [VMEM] * len(before),
        out_specs=VMEM,
        scratch_shapes=[
            pltpu.VMEM((count, 3 * LANES), jnp.float32),
            pltpu.VMEM((count // ROOTS, ROOTS, 3 * LANES), jnp.int32),
            pltpu.VMEM((count // ROOTS, 2, LANES), jnp.int32),
        ],
        input_output_aliases={3 + len(columns): 0} if before else {},
        compiler_params=pltpu.CompilerParams(vmem_limit_bytes=VMEM_LIMIT),
        cost_estimate=estimate(columns, rows),
    )(grp, slot_pair, rows, *columns, *before)


def total_kernel(received, out):
    width = 9 * LANES
    total = jnp.zeros((2, width), jnp.float32)
    for sender in range(received.shape[0]):
        exponent = received[sender, :, width:].astype(jnp.int32).astype(jnp.float32)
        unit = jnp.concatenate([jnp.exp2(exponent) * (1.0 / STEPS)] * 9, axis=1)
        steps = received[sender, :, :width].astype(jnp.int32).astype(jnp.float32)
        total = total + steps * unit
    for j in range(ROOTS // 2):
        two = slice(2 * j, 2 * j + 2)
        out[two, :LANES] = total[:, j * LANES : (j + 1) * LANES]
        out[two, LANES : 2 * LANES] = total[:, (4 + j) * LANES : (5 + j) * LANES]
        tail = total[:, 8 * LANES :]
        tail = tail if j == 0 else pltpu.roll(tail, LANES - j * TAIL, 1)
        out[two, 2 * LANES :] = tail[:, :TAIL]


def add_received(received, rows):
    return pl.pallas_call(
        total_kernel,
        out_shape=jax.ShapeDtypeStruct((ROOTS, rows), jnp.float32),
        in_specs=[VMEM],
        out_specs=VMEM,
        compiler_params=pltpu.CompilerParams(vmem_limit_bytes=VMEM_LIMIT),
    )(received)


def on_device(amplitudes, ladder, orbital_irrep, panel_rows, slot_pair):
    grp = lax.axis_index("grp").astype(jnp.int32).reshape(1)
    own = amplitudes.T
    mine = other_chip(own, 0)

    orbital_irrep, panel_rows = near_copies(orbital_irrep, panel_rows)
    col_sym = column_symmetry(orbital_irrep, ladder.shape[1])
    row_sym = jnp.bitwise_xor(
        lookup(panel_rows // V, orbital_irrep), lookup(panel_rows % V, orbital_irrep)
    )
    first, row_sym, col_sym = lax.optimization_barrier((own, row_sym, col_sym))
    theirs, own_other = other_chip(first, 1), other_core(first)
    mine, row_sym, col_sym = lax.optimization_barrier((mine, row_sym, col_sym))
    far = other_chip(mine, 1)
    masked = jnp.where(row_sym[:, None] == col_sym[None, :], ladder, jnp.zeros((), ladder.dtype))
    ordered = slot_products("first", grp, slot_pair, masked, (own, own_other, mine))
    mine, theirs, ordered = lax.optimization_barrier((mine, theirs, ordered))
    mine_other, theirs_other = other_core(mine), other_core(theirs)
    near = (theirs, mine_other, theirs_other)
    ordered = slot_products("second", grp, slot_pair, masked, near, ordered)
    far_other = other_core(far)
    ordered = slot_products("far", grp, slot_pair, masked, (far, far_other), ordered)
    received = lax.all_to_all(ordered, "ef", 0, 0, tiled=True)
    return add_received(received, ladder.shape[0]).T


def solution(mesh):
    in_specs = (P("ef", "grp"), P("grp", "ef"), P(), P("grp"), P())
    out_specs = P("grp", "ef")
    return jax.shard_map(
        on_device, mesh=mesh, in_specs=in_specs, out_specs=out_specs, check_vma=False
    )
```

```python
import functools

import jax
import jax.numpy as jnp
from jax import lax
from jax.experimental import pallas as pl
from jax.experimental.pallas import tpu as pltpu
from jax.sharding import PartitionSpec as P

V = 600
ROOTS = 8
N_X = 4
GROUP_SLOTS = 8
CHUNK = 1024
LANES = 128
TAIL = 32
STEPS = 32000.0
PAIRS = 64
STRIDE = 25
PLACE = pow(STRIDE, -1, PAIRS)
SMALLEST = 1e-30
VMEM_LIMIT = 10 << 20

VMEM = pl.BlockSpec(memory_space=pltpu.VMEM)
SMEM = pl.BlockSpec(memory_space=pltpu.SMEM)


def lookup(indices, orbital_irrep):
    orbitals = jnp.arange(orbital_irrep.shape[0], dtype=jnp.int32)
    return jnp.max(
        jnp.where(indices[:, None] == orbitals[None, :], orbital_irrep[None, :], 0), axis=1
    )


def copy_kernel(*refs):
    for source, out in zip(refs[: len(refs) // 2], refs[len(refs) // 2 :], strict=True):
        out[...] = source[...]


def near_copies(*tables):
    return pl.pallas_call(
        copy_kernel,
        out_shape=[jax.ShapeDtypeStruct(t.shape, t.dtype) for t in tables],
        in_specs=[VMEM] * len(tables),
        out_specs=[VMEM] * len(tables),
        compiler_params=pltpu.CompilerParams(vmem_limit_bytes=VMEM_LIMIT),
        cost_estimate=pl.CostEstimate(flops=0, bytes_accessed=4096, transcendentals=0),
    )(*tables)


def column_symmetry(orbital_irrep, width):
    offset = lax.axis_index("ef") * width
    count = (V - 1 + width) // V + 1
    first = offset // V
    padded = jnp.concatenate([orbital_irrep, jnp.zeros((count,), jnp.int32)])
    outer = lax.dynamic_slice(padded, (first,), (count,))
    table = jnp.bitwise_xor(outer[:, None], orbital_irrep[None, :]).reshape(count * V)
    return lax.dynamic_slice(table, (offset - first * V,), (width,))


def neighbour(x, c):
    return (N_X - 1 - x) * c + (x + 1 - 2 * (x % 2)) * (1 - c)


def other_chip(value, link):
    pairs = [(x * 2 + c, neighbour(x, c ^ link) * 2 + c) for x in range(N_X) for c in range(2)]
    return lax.ppermute(value, "grp", pairs)


def other_core(value):
    return lax.ppermute(value, "grp", [(g, g ^ 1) for g in range(2 * N_X)])


def product(columns, rows):
    width = rows.shape[1]
    total = None
    for low in range(0, width, CHUNK):
        span = slice(low, min(low + CHUNK, width))
        left = jnp.concatenate([c[:, span] for c in columns], axis=0)
        part = lax.dot_general(
            rows[:, span], left, (((1,), (1,)), ((), ())), preferred_element_type=jnp.float32
        )
        total = part if total is None else total + part
    return total.T


def pack(out, pair, block, exponent):
    lane = lax.broadcasted_iota(jnp.int32, (2, LANES), 1)
    tail = block[:2, 2 * LANES :]
    for j in range(1, ROOTS // 2):
        piece = pltpu.roll(block[2 * j : 2 * j + 2, 2 * LANES :], j * TAIL, 1)
        tail = jnp.where(lane >= j * TAIL, piece, tail)
    pieces = [block[2 * j : 2 * j + 2, :LANES] for j in range(ROOTS // 2)]
    pieces += [block[2 * j : 2 * j + 2, LANES : 2 * LANES] for j in range(ROOTS // 2)]
    out[pair] = jnp.concatenate(pieces + [tail, exponent], axis=1).astype(out.dtype)


def store_slots(grp, slot_pair, owners, held, steps, exponents, out):
    count = held.shape[0] // ROOTS
    values = held[...].reshape(count, ROOTS, held.shape[1])
    largest = jnp.max(jnp.max(jnp.abs(values), axis=1, keepdims=True), axis=2, keepdims=True)
    exponent = jnp.floor(jnp.log2(jnp.maximum(largest, SMALLEST))) + 1.0
    scale = jnp.exp2(-exponent) * STEPS
    steps[...] = jnp.round(values * scale).astype(jnp.int32)
    exponents[...] = jnp.broadcast_to(exponent, exponents.shape).astype(jnp.int32)
    for block, (chip, core) in enumerate(owners):
        group = lax.rem(chip, N_X) * 2 + core
        for slot in range(GROUP_SLOTS):
            pair = lax.rem(slot_pair[group * GROUP_SLOTS + slot] * PLACE, PAIRS)
            index = block * GROUP_SLOTS + slot
            pack(out, pair, steps[index], exponents[index])


def owners_of(grp, part):
    x, c = grp[0] // 2, grp[0] % 2
    a, b = neighbour(x, c), neighbour(x, 1 - c)
    if part == "first":
        return (x, c), (x, 1 - c), (a, c)
    if part == "second":
        return (b, c), (b, 1 - c), (a, 1 - c)
    return (x + 2, c), (x + 2, 1 - c)


def product_kernel(part, grp, slot_pair, rows, *refs):
    owners = owners_of(grp, part)
    out, held, steps, exponents = refs[-4:]
    count = rows.shape[0]
    held[:, 2 * LANES :] = jnp.zeros((held.shape[0], LANES), held.dtype)
    held[:, :count] = product(refs[: len(owners)], rows)
    store_slots(grp, slot_pair, owners, held, steps, exponents, out)


def estimate(columns, rows):
    count = sum(c.shape[0] for c in columns)
    return pl.CostEstimate(
        flops=8 * count * rows.shape[0] * rows.shape[1],
        bytes_accessed=2 * rows.shape[1] * (count + rows.shape[0]),
        transcendentals=0,
    )


def slot_products(part, grp, slot_pair, rows, columns, ordered=None):
    count = sum(c.shape[0] for c in columns)
    before = [] if ordered is None else [ordered]
    return pl.pallas_call(
        functools.partial(product_kernel, part),
        out_shape=jax.ShapeDtypeStruct((slot_pair.shape[0], 2, 10 * LANES), jnp.int16),
        in_specs=[SMEM, SMEM, VMEM] + [VMEM] * len(columns) + [VMEM] * len(before),
        out_specs=VMEM,
        scratch_shapes=[
            pltpu.VMEM((count, 3 * LANES), jnp.float32),
            pltpu.VMEM((count // ROOTS, ROOTS, 3 * LANES), jnp.int32),
            pltpu.VMEM((count // ROOTS, 2, LANES), jnp.int32),
        ],
        input_output_aliases={3 + len(columns): 0} if before else {},
        compiler_params=pltpu.CompilerParams(vmem_limit_bytes=VMEM_LIMIT),
        cost_estimate=estimate(columns, rows),
    )(grp, slot_pair, rows, *columns, *before)


def total_kernel(received, out):
    width = 9 * LANES
    total = jnp.zeros((2, width), jnp.float32)
    for sender in range(received.shape[0]):
        exponent = received[sender, :, width:].astype(jnp.int32).astype(jnp.float32)
        unit = jnp.concatenate([jnp.exp2(exponent) * (1.0 / STEPS)] * 9, axis=1)
        steps = received[sender, :, :width].astype(jnp.int32).astype(jnp.float32)
        total = total + steps * unit
    for j in range(ROOTS // 2):
        two = slice(2 * j, 2 * j + 2)
        out[two, :LANES] = total[:, j * LANES : (j + 1) * LANES]
        out[two, LANES : 2 * LANES] = total[:, (4 + j) * LANES : (5 + j) * LANES]
        tail = total[:, 8 * LANES :]
        tail = tail if j == 0 else pltpu.roll(tail, LANES - j * TAIL, 1)
        out[two, 2 * LANES :] = tail[:, :TAIL]


def add_received(received, rows):
    return pl.pallas_call(
        total_kernel,
        out_shape=jax.ShapeDtypeStruct((ROOTS, rows), jnp.float32),
        in_specs=[VMEM],
        out_specs=VMEM,
        compiler_params=pltpu.CompilerParams(vmem_limit_bytes=VMEM_LIMIT),
    )(received)


def on_device(amplitudes, ladder, orbital_irrep, panel_rows, slot_pair):
    grp = lax.axis_index("grp").astype(jnp.int32).reshape(1)
    own = amplitudes.T
    mine = other_chip(own, 0)

    orbital_irrep, panel_rows = near_copies(orbital_irrep, panel_rows)
    col_sym = column_symmetry(orbital_irrep, ladder.shape[1])
    row_sym = jnp.bitwise_xor(
        lookup(panel_rows // V, orbital_irrep), lookup(panel_rows % V, orbital_irrep)
    )
    first, row_sym, col_sym = lax.optimization_barrier((own, row_sym, col_sym))
    theirs, own_other = other_chip(first, 1), other_core(first)
    mine, row_sym, col_sym = lax.optimization_barrier((mine, row_sym, col_sym))
    far = other_chip(mine, 1)
    masked = jnp.where(row_sym[:, None] == col_sym[None, :], ladder, jnp.zeros((), ladder.dtype))
    ordered = slot_products("first", grp, slot_pair, masked, (own, own_other, mine))
    mine, theirs, ordered = lax.optimization_barrier((mine, theirs, ordered))
    mine_other, theirs_other = other_core(mine), other_core(theirs)
    near = (theirs, mine_other, theirs_other)
    ordered = slot_products("second", grp, slot_pair, masked, near, ordered)
    far_other = other_core(far)
    ordered = slot_products("far", grp, slot_pair, masked, (far, far_other), ordered)
    members = [[i * STRIDE % PAIRS for i in range(PAIRS)]]
    received = lax.all_to_all(ordered, "ef", 0, 0, tiled=True, axis_index_groups=members)
    return add_received(received, ladder.shape[0]).T


def solution(mesh):
    in_specs = (P("ef", "grp"), P("grp", "ef"), P(), P("grp"), P())
    out_specs = P("grp", "ef")
    return jax.shard_map(
        on_device, mesh=mesh, in_specs=in_specs, out_specs=out_specs, check_vma=False
    )
```

```python
import functools

import jax
import jax.numpy as jnp
from jax import lax
from jax.experimental import pallas as pl
from jax.experimental.pallas import tpu as pltpu
from jax.sharding import PartitionSpec as P

V = 600
ROOTS = 8
N_X = 4
GROUP_SLOTS = 8
CHUNK = 1024
LANES = 128
TAIL = 32
STEPS = 32000.0
PAIRS = 64
STRIDE = 41
PLACE = pow(STRIDE, -1, PAIRS)
SMALLEST = 1e-30
VMEM_LIMIT = 10 << 20

VMEM = pl.BlockSpec(memory_space=pltpu.VMEM)
SMEM = pl.BlockSpec(memory_space=pltpu.SMEM)


def lookup(indices, orbital_irrep):
    orbitals = jnp.arange(orbital_irrep.shape[0], dtype=jnp.int32)
    return jnp.max(
        jnp.where(indices[:, None] == orbitals[None, :], orbital_irrep[None, :], 0), axis=1
    )


def copy_kernel(*refs):
    for source, out in zip(refs[: len(refs) // 2], refs[len(refs) // 2 :], strict=True):
        out[...] = source[...]


def near_copies(*tables):
    return pl.pallas_call(
        copy_kernel,
        out_shape=[jax.ShapeDtypeStruct(t.shape, t.dtype) for t in tables],
        in_specs=[VMEM] * len(tables),
        out_specs=[VMEM] * len(tables),
        compiler_params=pltpu.CompilerParams(vmem_limit_bytes=VMEM_LIMIT),
        cost_estimate=pl.CostEstimate(flops=0, bytes_accessed=4096, transcendentals=0),
    )(*tables)


def column_symmetry(orbital_irrep, width):
    offset = lax.axis_index("ef") * width
    count = (V - 1 + width) // V + 1
    first = offset // V
    padded = jnp.concatenate([orbital_irrep, jnp.zeros((count,), jnp.int32)])
    outer = lax.dynamic_slice(padded, (first,), (count,))
    table = jnp.bitwise_xor(outer[:, None], orbital_irrep[None, :]).reshape(count * V)
    return lax.dynamic_slice(table, (offset - first * V,), (width,))


def neighbour(x, c):
    return (N_X - 1 - x) * (1 - c) + (x + 1 - 2 * (x % 2)) * c


def other_chip(value, link):
    pairs = [(x * 2 + c, neighbour(x, c ^ link) * 2 + c) for x in range(N_X) for c in range(2)]
    return lax.ppermute(value, "grp", pairs)


def other_core(value):
    return lax.ppermute(value, "grp", [(g, g ^ 1) for g in range(2 * N_X)])


def product(columns, rows):
    width = rows.shape[1]
    total = None
    for low in range(0, width, CHUNK):
        span = slice(low, min(low + CHUNK, width))
        left = jnp.concatenate([c[:, span] for c in columns], axis=0)
        part = lax.dot_general(
            rows[:, span], left, (((1,), (1,)), ((), ())), preferred_element_type=jnp.float32
        )
        total = part if total is None else total + part
    return total.T


def pack(out, pair, block, exponent):
    lane = lax.broadcasted_iota(jnp.int32, (2, LANES), 1)
    tail = block[:2, 2 * LANES :]
    for j in range(1, ROOTS // 2):
        piece = pltpu.roll(block[2 * j : 2 * j + 2, 2 * LANES :], j * TAIL, 1)
        tail = jnp.where(lane >= j * TAIL, piece, tail)
    pieces = [block[2 * j : 2 * j + 2, :LANES] for j in range(ROOTS // 2)]
    pieces += [block[2 * j : 2 * j + 2, LANES : 2 * LANES] for j in range(ROOTS // 2)]
    out[pair] = jnp.concatenate(pieces + [tail, exponent], axis=1).astype(out.dtype)


def store_slots(grp, slot_pair, owners, held, steps, exponents, out):
    count = held.shape[0] // ROOTS
    values = held[...].reshape(count, ROOTS, held.shape[1])
    largest = jnp.max(jnp.max(jnp.abs(values), axis=1, keepdims=True), axis=2, keepdims=True)
    exponent = jnp.floor(jnp.log2(jnp.maximum(largest, SMALLEST))) + 1.0
    scale = jnp.exp2(-exponent) * STEPS
    steps[...] = jnp.round(values * scale).astype(jnp.int32)
    exponents[...] = jnp.broadcast_to(exponent, exponents.shape).astype(jnp.int32)
    for block, (chip, core) in enumerate(owners):
        group = lax.rem(chip, N_X) * 2 + core
        for slot in range(GROUP_SLOTS):
            pair = lax.rem(slot_pair[group * GROUP_SLOTS + slot] * PLACE, PAIRS)
            index = block * GROUP_SLOTS + slot
            pack(out, pair, steps[index], exponents[index])


def owners_of(grp, part):
    x, c = grp[0] // 2, grp[0] % 2
    a, b = neighbour(x, c), neighbour(x, 1 - c)
    if part == "first":
        return (x, c), (x, 1 - c), (a, c)
    if part == "second":
        return (b, c), (b, 1 - c), (a, 1 - c)
    return (x + 2, c), (x + 2, 1 - c)


def product_kernel(part, grp, slot_pair, rows, *refs):
    owners = owners_of(grp, part)
    out, held, steps, exponents = refs[-4:]
    count = rows.shape[0]
    held[:, 2 * LANES :] = jnp.zeros((held.shape[0], LANES), held.dtype)
    held[:, :count] = product(refs[: len(owners)], rows)
    store_slots(grp, slot_pair, owners, held, steps, exponents, out)


def estimate(columns, rows):
    count = sum(c.shape[0] for c in columns)
    return pl.CostEstimate(
        flops=8 * count * rows.shape[0] * rows.shape[1],
        bytes_accessed=2 * rows.shape[1] * (count + rows.shape[0]),
        transcendentals=0,
    )


def slot_products(part, grp, slot_pair, rows, columns, ordered=None):
    count = sum(c.shape[0] for c in columns)
    before = [] if ordered is None else [ordered]
    return pl.pallas_call(
        functools.partial(product_kernel, part),
        out_shape=jax.ShapeDtypeStruct((slot_pair.shape[0], 2, 10 * LANES), jnp.int16),
        in_specs=[SMEM, SMEM, VMEM] + [VMEM] * len(columns) + [VMEM] * len(before),
        out_specs=VMEM,
        scratch_shapes=[
            pltpu.VMEM((count, 3 * LANES), jnp.float32),
            pltpu.VMEM((count // ROOTS, ROOTS, 3 * LANES), jnp.int32),
            pltpu.VMEM((count // ROOTS, 2, LANES), jnp.int32),
        ],
        input_output_aliases={3 + len(columns): 0} if before else {},
        compiler_params=pltpu.CompilerParams(vmem_limit_bytes=VMEM_LIMIT),
        cost_estimate=estimate(columns, rows),
    )(grp, slot_pair, rows, *columns, *before)


def total_kernel(received, out):
    width = 9 * LANES
    total = jnp.zeros((2, width), jnp.float32)
    for sender in range(received.shape[0]):
        exponent = received[sender, :, width:].astype(jnp.int32).astype(jnp.float32)
        unit = jnp.concatenate([jnp.exp2(exponent) * (1.0 / STEPS)] * 9, axis=1)
        steps = received[sender, :, :width].astype(jnp.int32).astype(jnp.float32)
        total = total + steps * unit
    for j in range(ROOTS // 2):
        two = slice(2 * j, 2 * j + 2)
        out[two, :LANES] = total[:, j * LANES : (j + 1) * LANES]
        out[two, LANES : 2 * LANES] = total[:, (4 + j) * LANES : (5 + j) * LANES]
        tail = total[:, 8 * LANES :]
        tail = tail if j == 0 else pltpu.roll(tail, LANES - j * TAIL, 1)
        out[two, 2 * LANES :] = tail[:, :TAIL]


def add_received(received, rows):
    return pl.pallas_call(
        total_kernel,
        out_shape=jax.ShapeDtypeStruct((ROOTS, rows), jnp.float32),
        in_specs=[VMEM],
        out_specs=VMEM,
        compiler_params=pltpu.CompilerParams(vmem_limit_bytes=VMEM_LIMIT),
    )(received)


def on_device(amplitudes, ladder, orbital_irrep, panel_rows, slot_pair):
    grp = lax.axis_index("grp").astype(jnp.int32).reshape(1)
    own = amplitudes.T
    mine = other_chip(own, 0)

    orbital_irrep, panel_rows = near_copies(orbital_irrep, panel_rows)
    col_sym = column_symmetry(orbital_irrep, ladder.shape[1])
    row_sym = jnp.bitwise_xor(
        lookup(panel_rows // V, orbital_irrep), lookup(panel_rows % V, orbital_irrep)
    )
    first, row_sym, col_sym = lax.optimization_barrier((own, row_sym, col_sym))
    theirs, own_other = other_chip(first, 1), other_core(first)
    mine, row_sym, col_sym = lax.optimization_barrier((mine, row_sym, col_sym))
    far = other_chip(mine, 1)
    masked = jnp.where(row_sym[:, None] == col_sym[None, :], ladder, jnp.zeros((), ladder.dtype))
    ordered = slot_products("first", grp, slot_pair, masked, (own, own_other, mine))
    mine, theirs, ordered = lax.optimization_barrier((mine, theirs, ordered))
    mine_other, theirs_other = other_core(mine), other_core(theirs)
    near = (theirs, mine_other, theirs_other)
    ordered = slot_products("second", grp, slot_pair, masked, near, ordered)
    far_other = other_core(far)
    ordered = slot_products("far", grp, slot_pair, masked, (far, far_other), ordered)
    members = [[i * STRIDE % PAIRS for i in range(PAIRS)]]
    received = lax.all_to_all(ordered, "ef", 0, 0, tiled=True, axis_index_groups=members)
    return add_received(received, ladder.shape[0]).T


def solution(mesh):
    in_specs = (P("ef", "grp"), P("grp", "ef"), P(), P("grp"), P())
    out_specs = P("grp", "ef")
    return jax.shard_map(
        on_device, mesh=mesh, in_specs=in_specs, out_specs=out_specs, check_vma=False
    )
```

```python
import functools

import jax
import jax.numpy as jnp
from jax import lax
from jax.experimental import pallas as pl
from jax.experimental.pallas import tpu as pltpu
from jax.sharding import PartitionSpec as P

V = 600
ROOTS = 8
N_X = 4
GROUP_SLOTS = 8
CHUNK = 1024
LANES = 128
TAIL = 32
PAIRS = 64
STRIDE = 41
PLACE = pow(STRIDE, -1, PAIRS)
VMEM_LIMIT = 10 << 20

VMEM = pl.BlockSpec(memory_space=pltpu.VMEM)
SMEM = pl.BlockSpec(memory_space=pltpu.SMEM)


def lookup(indices, orbital_irrep):
    orbitals = jnp.arange(orbital_irrep.shape[0], dtype=jnp.int32)
    return jnp.max(
        jnp.where(indices[:, None] == orbitals[None, :], orbital_irrep[None, :], 0), axis=1
    )


def copy_kernel(*refs):
    for source, out in zip(refs[: len(refs) // 2], refs[len(refs) // 2 :], strict=True):
        out[...] = source[...]


def near_copies(*tables):
    return pl.pallas_call(
        copy_kernel,
        out_shape=[jax.ShapeDtypeStruct(t.shape, t.dtype) for t in tables],
        in_specs=[VMEM] * len(tables),
        out_specs=[VMEM] * len(tables),
        compiler_params=pltpu.CompilerParams(vmem_limit_bytes=VMEM_LIMIT),
        cost_estimate=pl.CostEstimate(flops=0, bytes_accessed=4096, transcendentals=0),
    )(*tables)


def column_symmetry(orbital_irrep, width):
    offset = lax.axis_index("ef") * width
    count = (V - 1 + width) // V + 1
    first = offset // V
    padded = jnp.concatenate([orbital_irrep, jnp.zeros((count,), jnp.int32)])
    outer = lax.dynamic_slice(padded, (first,), (count,))
    table = jnp.bitwise_xor(outer[:, None], orbital_irrep[None, :]).reshape(count * V)
    return lax.dynamic_slice(table, (offset - first * V,), (width,))


def neighbour(x, c):
    return (N_X - 1 - x) * (1 - c) + (x + 1 - 2 * (x % 2)) * c


def other_chip(value, link):
    pairs = [(x * 2 + c, neighbour(x, c ^ link) * 2 + c) for x in range(N_X) for c in range(2)]
    return lax.ppermute(value, "grp", pairs)


def other_core(value):
    return lax.ppermute(value, "grp", [(g, g ^ 1) for g in range(2 * N_X)])


def product(columns, rows):
    width = rows.shape[1]
    total = None
    for low in range(0, width, CHUNK):
        span = slice(low, min(low + CHUNK, width))
        left = jnp.concatenate([c[:, span] for c in columns], axis=0)
        part = lax.dot_general(
            rows[:, span], left, (((1,), (1,)), ((), ())), preferred_element_type=jnp.float32
        )
        total = part if total is None else total + part
    return total.T


def pack(out, pair, block):
    lane = lax.broadcasted_iota(jnp.int32, (2, LANES), 1)
    tail = block[:2, 2 * LANES :]
    for j in range(1, ROOTS // 2):
        piece = pltpu.roll(block[2 * j : 2 * j + 2, 2 * LANES :], j * TAIL, 1)
        tail = jnp.where(lane >= j * TAIL, piece, tail)
    pieces = [block[2 * j : 2 * j + 2, :LANES] for j in range(ROOTS // 2)]
    pieces += [block[2 * j : 2 * j + 2, LANES : 2 * LANES] for j in range(ROOTS // 2)]
    out[pair] = jnp.concatenate(pieces + [tail], axis=1)


def store_slots(grp, slot_pair, owners, held, out):
    for block, (chip, core) in enumerate(owners):
        group = lax.rem(chip, N_X) * 2 + core
        for slot in range(GROUP_SLOTS):
            pair = lax.rem(slot_pair[group * GROUP_SLOTS + slot] * PLACE, PAIRS)
            pack(out, pair, held[pl.ds((block * GROUP_SLOTS + slot) * ROOTS, ROOTS), :])


def owners_of(grp, part):
    x, c = grp[0] // 2, grp[0] % 2
    a, b = neighbour(x, c), neighbour(x, 1 - c)
    if part == "first":
        return (x, c), (x, 1 - c), (a, c)
    if part == "second":
        return (b, c), (b, 1 - c), (a, 1 - c)
    return (x + 2, c), (x + 2, 1 - c)


def product_kernel(part, grp, slot_pair, rows, *refs):
    owners = owners_of(grp, part)
    out, held = refs[-2:]
    count = rows.shape[0]
    held[:, 2 * LANES :] = jnp.zeros((held.shape[0], LANES), held.dtype)
    held[:, :count] = product(refs[: len(owners)], rows)
    store_slots(grp, slot_pair, owners, held, out)


def estimate(columns, rows):
    count = sum(c.shape[0] for c in columns)
    return pl.CostEstimate(
        flops=8 * count * rows.shape[0] * rows.shape[1],
        bytes_accessed=2 * rows.shape[1] * (count + rows.shape[0]),
        transcendentals=0,
    )


def slot_products(part, grp, slot_pair, rows, columns, ordered=None):
    count = sum(c.shape[0] for c in columns)
    before = [] if ordered is None else [ordered]
    return pl.pallas_call(
        functools.partial(product_kernel, part),
        out_shape=jax.ShapeDtypeStruct((slot_pair.shape[0], 2, 9 * LANES), jnp.float32),
        in_specs=[SMEM, SMEM, VMEM] + [VMEM] * len(columns) + [VMEM] * len(before),
        out_specs=VMEM,
        scratch_shapes=[pltpu.VMEM((count, 3 * LANES), jnp.float32)],
        input_output_aliases={3 + len(columns): 0} if before else {},
        compiler_params=pltpu.CompilerParams(vmem_limit_bytes=VMEM_LIMIT),
        cost_estimate=estimate(columns, rows),
    )(grp, slot_pair, rows, *columns, *before)


def total_kernel(received, out):
    total = received[0]
    for sender in range(1, received.shape[0]):
        total = total + received[sender]
    for j in range(ROOTS // 2):
        two = slice(2 * j, 2 * j + 2)
        out[two, :LANES] = total[:, j * LANES : (j + 1) * LANES]
        out[two, LANES : 2 * LANES] = total[:, (4 + j) * LANES : (5 + j) * LANES]
        tail = total[:, 8 * LANES :]
        tail = tail if j == 0 else pltpu.roll(tail, LANES - j * TAIL, 1)
        out[two, 2 * LANES :] = tail[:, :TAIL]


def add_received(received, rows):
    return pl.pallas_call(
        total_kernel,
        out_shape=jax.ShapeDtypeStruct((ROOTS, rows), jnp.float32),
        in_specs=[VMEM],
        out_specs=VMEM,
        compiler_params=pltpu.CompilerParams(vmem_limit_bytes=VMEM_LIMIT),
    )(received)


def on_device(amplitudes, ladder, orbital_irrep, panel_rows, slot_pair):
    grp = lax.axis_index("grp").astype(jnp.int32).reshape(1)
    own = amplitudes.T
    mine = other_chip(own, 0)

    orbital_irrep, panel_rows = near_copies(orbital_irrep, panel_rows)
    col_sym = column_symmetry(orbital_irrep, ladder.shape[1])
    row_sym = jnp.bitwise_xor(
        lookup(panel_rows // V, orbital_irrep), lookup(panel_rows % V, orbital_irrep)
    )
    first, row_sym, col_sym = lax.optimization_barrier((own, row_sym, col_sym))
    theirs, own_other = other_chip(first, 1), other_core(first)
    mine, row_sym, col_sym = lax.optimization_barrier((mine, row_sym, col_sym))
    far = other_chip(mine, 1)
    masked = jnp.where(row_sym[:, None] == col_sym[None, :], ladder, jnp.zeros((), ladder.dtype))
    ordered = slot_products("first", grp, slot_pair, masked, (own, own_other, mine))
    mine, theirs, ordered = lax.optimization_barrier((mine, theirs, ordered))
    mine_other, theirs_other = other_core(mine), other_core(theirs)
    near = (theirs, mine_other, theirs_other)
    ordered = slot_products("second", grp, slot_pair, masked, near, ordered)
    far_other = other_core(far)
    ordered = slot_products("far", grp, slot_pair, masked, (far, far_other), ordered)
    members = [[i * STRIDE % PAIRS for i in range(PAIRS)]]
    received = lax.all_to_all(ordered, "ef", 0, 0, tiled=True, axis_index_groups=members)
    return add_received(received, ladder.shape[0]).T


def solution(mesh):
    in_specs = (P("ef", "grp"), P("grp", "ef"), P(), P("grp"), P())
    out_specs = P("grp", "ef")
    return jax.shard_map(
        on_device, mesh=mesh, in_specs=in_specs, out_specs=out_specs, check_vma=False
    )
```

```python
import functools

import jax
import jax.numpy as jnp
from jax import lax
from jax.experimental import pallas as pl
from jax.experimental.pallas import tpu as pltpu
from jax.sharding import PartitionSpec as P

V = 600
ROOTS = 8
N_X = 4
GROUP_SLOTS = 8
CHUNK = 1024
LANES = 128
TAIL = 32
STEPS = 32000.0
PAIRS = 64
STRIDE = 41
PLACE = pow(STRIDE, -1, PAIRS)
SMALLEST = 1e-30
VMEM_LIMIT = 10 << 20

VMEM = pl.BlockSpec(memory_space=pltpu.VMEM)
SMEM = pl.BlockSpec(memory_space=pltpu.SMEM)


def lookup(indices, orbital_irrep):
    orbitals = jnp.arange(orbital_irrep.shape[0], dtype=jnp.int32)
    return jnp.max(
        jnp.where(indices[:, None] == orbitals[None, :], orbital_irrep[None, :], 0), axis=1
    )


def copy_kernel(*refs):
    for source, out in zip(refs[: len(refs) // 2], refs[len(refs) // 2 :], strict=True):
        out[...] = source[...]


def near_copies(*tables):
    return pl.pallas_call(
        copy_kernel,
        out_shape=[jax.ShapeDtypeStruct(t.shape, t.dtype) for t in tables],
        in_specs=[VMEM] * len(tables),
        out_specs=[VMEM] * len(tables),
        compiler_params=pltpu.CompilerParams(vmem_limit_bytes=VMEM_LIMIT),
        cost_estimate=pl.CostEstimate(flops=0, bytes_accessed=4096, transcendentals=0),
    )(*tables)


def column_symmetry(orbital_irrep, width):
    offset = lax.axis_index("ef") * width
    count = (V - 1 + width) // V + 1
    first = offset // V
    padded = jnp.concatenate([orbital_irrep, jnp.zeros((count,), jnp.int32)])
    outer = lax.dynamic_slice(padded, (first,), (count,))
    table = jnp.bitwise_xor(outer[:, None], orbital_irrep[None, :]).reshape(count * V)
    return lax.dynamic_slice(table, (offset - first * V,), (width,))


def neighbour(x, c):
    return (N_X - 1 - x) * (1 - c) + (x + 1 - 2 * (x % 2)) * c


def other_chip(value, link):
    pairs = [(x * 2 + c, neighbour(x, c ^ link) * 2 + c) for x in range(N_X) for c in range(2)]
    return lax.ppermute(value, "grp", pairs)


def other_core(value):
    return lax.ppermute(value, "grp", [(g, g ^ 1) for g in range(2 * N_X)])


def product(columns, rows):
    width = rows.shape[1]
    total = None
    for low in range(0, width, CHUNK):
        span = slice(low, min(low + CHUNK, width))
        left = jnp.concatenate([c[:, span] for c in columns], axis=0)
        part = lax.dot_general(
            rows[:, span], left, (((1,), (1,)), ((), ())), preferred_element_type=jnp.float32
        )
        total = part if total is None else total + part
    return total.T


def pack(out, pair, block, exponent):
    lane = lax.broadcasted_iota(jnp.int32, (2, LANES), 1)
    tail = block[:2, 2 * LANES :]
    for j in range(1, ROOTS // 2):
        piece = pltpu.roll(block[2 * j : 2 * j + 2, 2 * LANES :], j * TAIL, 1)
        tail = jnp.where(lane >= j * TAIL, piece, tail)
    pieces = [block[2 * j : 2 * j + 2, :LANES] for j in range(ROOTS // 2)]
    pieces += [block[2 * j : 2 * j + 2, LANES : 2 * LANES] for j in range(ROOTS // 2)]
    out[pair] = jnp.concatenate(pieces + [tail, exponent], axis=1).astype(out.dtype)


def store_slots(grp, slot_pair, owners, held, steps, exponents, out):
    count = held.shape[0] // ROOTS
    values = held[...].reshape(count, ROOTS, held.shape[1])
    largest = jnp.max(jnp.max(jnp.abs(values), axis=1, keepdims=True), axis=2, keepdims=True)
    exponent = jnp.floor(jnp.log2(jnp.maximum(largest, SMALLEST))) + 1.0
    scale = jnp.exp2(-exponent) * STEPS
    steps[...] = jnp.round(values * scale).astype(jnp.int32)
    exponents[...] = jnp.broadcast_to(exponent, exponents.shape).astype(jnp.int32)
    for block, (chip, core) in enumerate(owners):
        group = lax.rem(chip, N_X) * 2 + core
        for slot in range(GROUP_SLOTS):
            pair = lax.rem(slot_pair[group * GROUP_SLOTS + slot] * PLACE, PAIRS)
            index = block * GROUP_SLOTS + slot
            pack(out, pair, steps[index], exponents[index])


def owners_of(grp, part):
    x, c = grp[0] // 2, grp[0] % 2
    a, b = neighbour(x, c), neighbour(x, 1 - c)
    if part == "first":
        return (x, c), (x, 1 - c), (a, c)
    if part == "second":
        return (b, c), (b, 1 - c), (a, 1 - c)
    return (x + 2, c), (x + 2, 1 - c)


def product_kernel(part, grp, slot_pair, rows, *refs):
    owners = owners_of(grp, part)
    out, held, steps, exponents = refs[-4:]
    count = rows.shape[0]
    held[:, 2 * LANES :] = jnp.zeros((held.shape[0], LANES), held.dtype)
    held[:, :count] = product(refs[: len(owners)], rows)
    store_slots(grp, slot_pair, owners, held, steps, exponents, out)


def estimate(columns, rows):
    count = sum(c.shape[0] for c in columns)
    return pl.CostEstimate(
        flops=8 * count * rows.shape[0] * rows.shape[1],
        bytes_accessed=2 * rows.shape[1] * (count + rows.shape[0]),
        transcendentals=0,
    )


def slot_products(part, grp, slot_pair, rows, columns, ordered=None):
    count = sum(c.shape[0] for c in columns)
    before = [] if ordered is None else [ordered]
    return pl.pallas_call(
        functools.partial(product_kernel, part),
        out_shape=jax.ShapeDtypeStruct((slot_pair.shape[0], 2, 10 * LANES), jnp.int16),
        in_specs=[SMEM, SMEM, VMEM] + [VMEM] * len(columns) + [VMEM] * len(before),
        out_specs=VMEM,
        scratch_shapes=[
            pltpu.VMEM((count, 3 * LANES), jnp.float32),
            pltpu.VMEM((count // ROOTS, ROOTS, 3 * LANES), jnp.int32),
            pltpu.VMEM((count // ROOTS, 2, LANES), jnp.int32),
        ],
        input_output_aliases={3 + len(columns): 0} if before else {},
        compiler_params=pltpu.CompilerParams(vmem_limit_bytes=VMEM_LIMIT),
        cost_estimate=estimate(columns, rows),
    )(grp, slot_pair, rows, *columns, *before)


def total_kernel(received, out):
    width = 9 * LANES
    total = jnp.zeros((2, width), jnp.float32)
    for sender in range(received.shape[0]):
        exponent = received[sender, :, width:].astype(jnp.int32).astype(jnp.float32)
        unit = jnp.concatenate([jnp.exp2(exponent) * (1.0 / STEPS)] * 9, axis=1)
        steps = received[sender, :, :width].astype(jnp.int32).astype(jnp.float32)
        total = total + steps * unit
    for j in range(ROOTS // 2):
        two = slice(2 * j, 2 * j + 2)
        out[two, :LANES] = total[:, j * LANES : (j + 1) * LANES]
        out[two, LANES : 2 * LANES] = total[:, (4 + j) * LANES : (5 + j) * LANES]
        tail = total[:, 8 * LANES :]
        tail = tail if j == 0 else pltpu.roll(tail, LANES - j * TAIL, 1)
        out[two, 2 * LANES :] = tail[:, :TAIL]


def add_received(received, rows):
    return pl.pallas_call(
        total_kernel,
        out_shape=jax.ShapeDtypeStruct((ROOTS, rows), jnp.float32),
        in_specs=[VMEM],
        out_specs=VMEM,
        compiler_params=pltpu.CompilerParams(vmem_limit_bytes=VMEM_LIMIT),
    )(received)


def on_device(amplitudes, ladder, orbital_irrep, panel_rows, slot_pair):
    grp = lax.axis_index("grp").astype(jnp.int32).reshape(1)
    own = amplitudes.T
    mine = other_chip(own, 0)

    (orbital_irrep,) = near_copies(orbital_irrep)
    col_sym = column_symmetry(orbital_irrep, ladder.shape[1])
    first, col_sym = lax.optimization_barrier((own, col_sym))
    theirs, own_other = other_chip(first, 1), other_core(first)
    mine, col_sym = lax.optimization_barrier((mine, col_sym))
    far = other_chip(mine, 1)
    row_sym = jnp.bitwise_xor(
        lookup(panel_rows // V, orbital_irrep), lookup(panel_rows % V, orbital_irrep)
    )
    masked = jnp.where(row_sym[:, None] == col_sym[None, :], ladder, jnp.zeros((), ladder.dtype))
    ordered = slot_products("first", grp, slot_pair, masked, (own, own_other, mine))
    mine, theirs, ordered = lax.optimization_barrier((mine, theirs, ordered))
    mine_other, theirs_other = other_core(mine), other_core(theirs)
    near = (theirs, mine_other, theirs_other)
    ordered = slot_products("second", grp, slot_pair, masked, near, ordered)
    far_other = other_core(far)
    ordered = slot_products("far", grp, slot_pair, masked, (far, far_other), ordered)
    members = [[i * STRIDE % PAIRS for i in range(PAIRS)]]
    received = lax.all_to_all(ordered, "ef", 0, 0, tiled=True, axis_index_groups=members)
    return add_received(received, ladder.shape[0]).T


def solution(mesh):
    in_specs = (P("ef", "grp"), P("grp", "ef"), P(), P("grp"), P())
    out_specs = P("grp", "ef")
    return jax.shard_map(
        on_device, mesh=mesh, in_specs=in_specs, out_specs=out_specs, check_vma=False
    )
```
